32 devices in a mesh: groups: 2 (over x), tm: 16 (over z, y, core).
Axes of the slice: x: 2, y: 2, z: 4, core: 2. Of those that a mesh axis runs over, the one named last changes fastest.
Arguments:
- lin_mean: float32 [128, 512], P(('groups', 'tm')), parts along dimension 0, may hold values from -6 to 6
- spread: float32 [128, 512], P(('groups', 'tm')), parts along dimension 0, may hold values from 0.05 to 0.5
- keep: float32 [128, 512], P(('groups', 'tm')), parts along dimension 0, may hold values from 0.3 to 1
- observed: float32 [128, 512], P(('groups', 'tm')), parts along dimension 0, may hold values from -6 to 6
- start: float32 [1024], P('groups'), parts along dimension 0, may hold values from -6 to 6
- w_in: bfloat16 [512, 2048], replicated, may hold values from -0.176776695 to 0.176776695
- b_in: float32 [2048], replicated, may hold values from -3 to 3
- w_out: bfloat16 [2048, 512], replicated, may hold values from -0.013258252 to 0.013258252
- b_out: float32 [512], replicated, may hold values from -0.6 to 0.6
Outputs:
- filtered: float32 [128, 512], P(('groups', 'tm')), parts along dimension 0
The draws below stay inside these ranges and needn't reach their ends.
There are 2 independent parts, one for each index of `groups`. The reference program is written for one: setup_inputs(seed, part) draws one part's arguments, and reference() takes and returns one part's arrays. A program takes and returns all parts, laid end to end along the dimension named above; an argument that names none is the same for every part. Nothing has to cross between parts.
All inputs are finite; a program needn't handle non-finite values.
Results may differ from the reference program's by a relative error of at most 0.0003.
The reference program's roundings to bfloat16 on the way (of `points` and `hidden`) count: a program that leaves them out, or rounds other values in their place, can miss the bound.
Values sent between devices are 32-bit elements; how exact they have to be, the bound alone decides.
No kernel may reach another device: no remote copies, remote signals or barrier semaphores. Data moves between devices by JAX's collectives and lax.ppermute only.
A program may use at most 64 MiB of HBM per device.

```python
import math
import jax
import jax.numpy as jnp
from jax import lax

STATE_SIZE = 512
UNITS = 2048
TIME_STEP_COUNT = 64


def shared_layer(key):
    base = jnp.clip(jax.random.normal(key, (STATE_SIZE, UNITS), jnp.float32), -4.0, 4.0)
    return base * (1.0 / math.sqrt(STATE_SIZE))


def draw_w_in(key, part):
    return shared_layer(key).astype(jnp.bfloat16)


def draw_w_out(key, part):
    shared = shared_layer(key)
    key = jax.random.fold_in(key, 5)
    noise = jnp.clip(jax.random.normal(key, (UNITS, STATE_SIZE), jnp.float32), -4.0, 4.0)
    return (-0.035 * jnp.transpose(shared) + 0.08 / math.sqrt(UNITS) * noise).astype(jnp.bfloat16)


def draw_keep(key, part):
    key = jax.random.fold_in(key, 11)
    rate_key, roughness_key, surge_key, depth_key = jax.random.split(key, 4)
    lowest = 0.25 / TIME_STEP_COUNT
    highest = 0.03
    log_rate = jax.random.uniform(rate_key, (STATE_SIZE,), jnp.float32, math.log(lowest), math.log(highest))
    damping_rates = jnp.exp(log_rate)
    roughness_factor = jax.random.uniform(roughness_key, (TIME_STEP_COUNT, STATE_SIZE), jnp.float32, 0.5, 2.0)
    surge_strike = jax.random.uniform(surge_key, (TIME_STEP_COUNT, STATE_SIZE), jnp.float32)
    surge_depth = jax.random.uniform(depth_key, (TIME_STEP_COUNT, STATE_SIZE), jnp.float32, 0.32, 0.8)
    surge_factor = jnp.where(surge_strike < 3.0 / TIME_STEP_COUNT, surge_depth, 1.0)
    return jnp.exp(-damping_rates[None, :] * roughness_factor) * surge_factor


def levels(own_key, shape, cuts, least, largest):
    level = 1.0
    for axis_at, parts in cuts:
        draws = jax.random.uniform(jax.random.fold_in(jax.random.fold_in(own_key, 6), axis_at), (parts,), jnp.float32, least / len(cuts), largest / len(cuts))
        level = level * jnp.repeat(jnp.exp(draws), shape[axis_at] // parts).reshape((-1,) + (1,) * (len(shape) - 1 - axis_at))
    return level


def normal_values(rng, extent, width, most, cuts=(), kind=jnp.bfloat16):
    array = jax.random.normal(rng, extent, jnp.float32) * width
    if len(cuts) > 0:
        array = levels(rng, extent, cuts, -0.22, 0.18) * array
    return jnp.clip(array, min=-most, max=most).astype(kind)


def setup_inputs(seed: int = 0, part: int = 0) -> dict:
    key_of = jax.random.split(jax.random.key(seed), 10)
    own_keys = jax.random.split(jax.random.fold_in(key_of[9], part), 10)
    return {
        "lin_mean": normal_values(own_keys[0], (TIME_STEP_COUNT, STATE_SIZE), 1.0, 6.0, ((0, 16),), jnp.float32),
        "spread": jnp.clip(jnp.exp(math.log(0.5) - 2.3025851 * jax.random.uniform(own_keys[1], (TIME_STEP_COUNT, STATE_SIZE), jnp.float32) ** levels(own_keys[1], (TIME_STEP_COUNT, STATE_SIZE), ((0, 16),), -0.2, 0.2)), 0.05, 0.5),
        "keep": draw_keep(jax.random.fold_in(jax.random.fold_in(key_of[9], part), 71), part),
        "observed": normal_values(own_keys[3], (TIME_STEP_COUNT, STATE_SIZE), 1.0, 6.0, ((0, 16),), jnp.float32),
        "start": normal_values(own_keys[4], (STATE_SIZE,), 1.0, 6.0, (), jnp.float32),
        "w_in": draw_w_in(jax.random.fold_in(key_of[9], 71), part),
        "b_in": normal_values(key_of[6], (UNITS,), 0.5, 3.0, (), jnp.float32),
        "w_out": draw_w_out(jax.random.fold_in(key_of[9], 71), part),
        "b_out": normal_values(key_of[8], (STATE_SIZE,), 0.1, 0.6, (), jnp.float32),
    }


def forward_net(points, w_in, b_in, w_out, b_out):
    hidden = jax.nn.gelu(jnp.dot(points, w_in, preferred_element_type=jnp.float32) + b_in, approximate=True).astype(jnp.bfloat16)
    return jnp.dot(hidden, w_out, preferred_element_type=jnp.float32) + b_out + points.astype(jnp.float32)

def reference(lin_mean, spread, keep, observed, start, w_in, b_in, w_out, b_out):
    factor = math.sqrt(STATE_SIZE + 1.0)
    identity = jnp.eye(STATE_SIZE, dtype=jnp.float32)

    def advance(filt_prev, inputs):
        lin_row, spread_row, keep_row, observed_row = inputs
        offset = identity * (factor * spread_row)[:, None]
        upper_pts = (lin_row[None, :] + offset).astype(jnp.bfloat16)
        lower_pts = (lin_row[None, :] - offset).astype(jnp.bfloat16)
        upper_out = forward_net(upper_pts, w_in, b_in, w_out, b_out)
        lower_out = forward_net(lower_pts, w_in, b_in, w_out, b_out)
        centre = forward_net(lin_row[None, :].astype(jnp.bfloat16), w_in, b_in, w_out, b_out)[0]
        jacobian = (upper_out - lower_out) / (2.0 * factor * spread_row)[:, None]
        point_mean = centre / (STATE_SIZE + 1.0) + lax.optimization_barrier(jnp.sum(upper_out + lower_out, axis=0)) / (2.0 * (STATE_SIZE + 1.0))
        predicted = point_mean + jnp.dot(filt_prev - lin_row, jacobian, precision=lax.Precision.HIGHEST)
        new_state = keep_row * predicted + (1.0 - keep_row) * observed_row
        return (new_state, new_state)
    unused_last, filtered = lax.scan(advance, start, (lin_mean, spread, keep, observed))
    return filtered
```

```python
import functools
import math

import jax
import jax.numpy as jnp
from jax import lax
from jax.experimental import pallas as pl
from jax.experimental.pallas import tpu as pltpu
from jax.sharding import PartitionSpec as P

C0 = math.sqrt(2.0 / math.pi)
C1 = 0.044715 * C0
LANES = 128
F32 = jnp.float32
BF16 = jnp.bfloat16
VMEM = pl.BlockSpec(memory_space=pltpu.VMEM)


def split(x):
    hi = x.astype(BF16)
    return hi, (x - hi.astype(F32)).astype(BF16)


def product(left, right):
    lhi, llo = split(left)
    rhi, rlo = split(right)
    return jnp.dot(
        jnp.concatenate([lhi, llo, lhi], axis=1),
        jnp.concatenate([rhi, rhi, rlo], axis=0),
        preferred_element_type=F32,
    )


def columns_of(row):
    width = row.shape[1]
    return [
        jnp.transpose(jnp.broadcast_to(row[:, b : b + LANES], (LANES, LANES)))
        for b in range(0, width, LANES)
    ]


def row_times(cols, matrix):
    width = len(cols) * LANES
    parts = []
    for c in range(0, width, LANES):
        total = None
        for b in range(len(cols)):
            term = jnp.sum(
                (cols[b] * matrix(pl.ds(b * LANES, LANES), pl.ds(c, LANES))).reshape(LANES // 8, 8, LANES),
                axis=0,
            )
            total = term if total is None else total + term
        parts.append(jnp.sum(total, axis=0, keepdims=True))
    return jnp.concatenate(parts, axis=1)


def net_kernel(
    mean_ref, spread_ref, keep_ref, obs_ref, w_in, b_in, w_out, b_out,
    pre, last, offsets,
    base, wide, h0, h1, jac, pm,
):
    n_steps, width = mean_ref.shape
    units = w_in.shape[1]
    half = width // 2
    factor = math.sqrt(width + 1.0)
    mean = mean_ref[...]
    centre_pts = mean.astype(BF16)
    centre_f = centre_pts.astype(F32)
    base[...] = (jnp.dot(centre_pts, w_in[...], preferred_element_type=F32) + b_in[...]) * 0.5
    spread = spread_ref[...]
    up = (mean + factor * spread).astype(BF16).astype(F32)
    lo = (mean - factor * spread).astype(BF16).astype(F32)
    inv = 1.0 / (2.0 * factor * spread)
    for a, rows in enumerate((0.5 * (up - centre_f), 0.5 * (lo - centre_f), inv, (up - lo) * inv)):
        for k in range(n_steps):
            for b, block in enumerate(columns_of(rows[k : k + 1])):
                wide[a, k, pl.ds(b * LANES, LANES), :] = block

    def gelu(k, j0, dst):
        for c in range(0, units, 256):
            b = base[pl.ds(k, 1), pl.ds(c, 256)]
            for r in range(0, half, 16):
                w = w_in[pl.ds(j0 + r, 16), pl.ds(c, 256)].astype(F32)
                for s in range(2):
                    d = wide[s, k, pl.ds(j0 + r, 16), :]
                    y = b + jnp.concatenate([d, d], axis=1) * w
                    z = y * (y * y * (8.0 * C1) + 2.0 * C0)
                    dst[pl.ds(s * half + r, 16), pl.ds(c, 256)] = (y * jnp.tanh(z) + y).astype(BF16)

    def outer(k, j0, src):
        out = jnp.dot(src[...], w_out[...], preferred_element_type=F32)
        upper, lower = out[:half], out[half:]
        scale = wide[2, k, pl.ds(j0, half), :]
        own = wide[3, k, pl.ds(j0, half), :]
        keep = keep_ref[pl.ds(k, 1), :]
        rows = lax.broadcasted_iota(jnp.int32, (half, LANES), 0)
        lanes = lax.broadcasted_iota(jnp.int32, (half, LANES), 1)
        for c in range(0, width, LANES):
            v = (upper[:, c : c + LANES] - lower[:, c : c + LANES]) * scale
            if j0 <= c < j0 + half:
                v = v + jnp.where(rows == lanes + (c - j0), own, 0.0)
            jac[k, pl.ds(j0, half), pl.ds(c, LANES)] = v * keep[:, c : c + LANES]
        return jnp.sum(upper + lower, axis=0, keepdims=True)

    def step(k, carry):
        kp = jnp.maximum(k - 1, 0)
        total = outer(kp, half, h1)
        gelu(k, 0, h0)
        pm[pl.ds(kp, 1), :] = pm[pl.ds(kp, 1), :] + total
        total = outer(k, 0, h0)
        gelu(k, half, h1)
        pm[pl.ds(k, 1), :] = total
        return carry

    lax.fori_loop(0, n_steps, step, 0)
    pm[pl.ds(n_steps - 1, 1), :] = pm[pl.ds(n_steps - 1, 1), :] + outer(n_steps - 1, half, h1)

    points = 2.0 * width
    y = base[...]
    z = y * (y * y * (8.0 * C1) + 2.0 * C0)
    hidden = (y * jnp.tanh(z) + y).astype(BF16)
    centre = jnp.dot(hidden, w_out[...], preferred_element_type=F32) + b_out[...] + centre_f
    sums = pm[pl.ds(0, n_steps), :] + points * b_out[...] + ((points - 2.0) * centre_f + (up + lo))
    point_mean = centre / (width + 1.0) + sums / (2.0 * (width + 1.0))
    keep = keep_ref[...]
    free = keep * point_mean + (1.0 - keep) * obs_ref[...]
    consts = []
    for k in range(n_steps):
        moved = row_times(columns_of(mean[k : k + 1]), lambda r, c: jac[k, r, c])
        consts.append(free[k : k + 1] - moved)

    pad = jnp.zeros((7, width), F32)
    first = jac[0]
    pre[0] = first
    held = jnp.concatenate([first, consts[0], pad], axis=0)
    offsets[pl.ds(0, 1), :] = consts[0]
    for k in range(1, n_steps):
        held = product(held, jac[k])
        const = held[width : width + 1] + consts[k]
        offsets[pl.ds(k, 1), :] = const
        if k < n_steps - 1:
            pre[k] = held[:width]
            held = jnp.concatenate([held[:width], const, pad], axis=0)
        else:
            last[pl.ds(0, width), :] = held[:width]
            last[pl.ds(width, 8), :] = jnp.concatenate([const, pad], axis=0)


def pair_kernel(early, late, entry, chip, leaving):
    width = late.shape[1]
    both = product(early[...], late[pl.ds(0, width), :])
    chip[pl.ds(0, width), :] = both[:width]
    const = both[width : width + 1] + late[pl.ds(width, 1), :]
    chip[pl.ds(width, 8), :] = jnp.broadcast_to(const, (8, width))
    leaving[...] = row_times(columns_of(entry[...]), lambda r, c: chip[r, c]) + const


def hop_kernel(chip, entry, leaving):
    width = chip.shape[1]
    leaving[...] = row_times(columns_of(entry[...]), lambda r, c: chip[r, c]) + chip[pl.ds(width, 1), :]


def final_kernel(early, pre, last, offsets, entry, other, late_mask, out):
    n_steps, width = offsets.shape
    mid = row_times(columns_of(entry[...]), lambda r, c: early[r, c]) + early[pl.ds(width, 1), :]
    begin = jnp.where(late_mask[...] > 0.0, mid, other[...])
    cols = columns_of(begin)
    for k in range(n_steps):
        if k < n_steps - 1:
            moved = row_times(cols, lambda r, c: pre[k, r, c])
        else:
            moved = row_times(cols, lambda r, c: last[r, c])
        out[pl.ds(k, 1), :] = moved + offsets[pl.ds(k, 1), :]


def params():
    return pltpu.CompilerParams(vmem_limit_bytes=48 * 1024 * 1024)


def body(lin_mean, spread, keep, observed, start, w_in, b_in, w_out, b_out):
    n_steps, width = lin_mean.shape
    units = w_in.shape[1]
    size = lax.axis_size("tm")
    position = lax.axis_index("tm")
    shape = jax.ShapeDtypeStruct

    pre, last, offsets = pl.pallas_call(
        net_kernel,
        out_shape=(
            shape((n_steps - 1, width, width), F32),
            shape((width + 8, width), F32),
            shape((n_steps, width), F32),
        ),
        in_specs=[VMEM] * 8,
        out_specs=(VMEM,) * 3,
        scratch_shapes=[
            pltpu.VMEM((n_steps, units), F32),
            pltpu.VMEM((4, n_steps, width, LANES), F32),
            pltpu.VMEM((width, units), BF16),
            pltpu.VMEM((width, units), BF16),
            pltpu.VMEM((n_steps, width, width), F32),
            pltpu.VMEM((8, width), F32),
        ],
        compiler_params=params(),
    )(lin_mean, spread, keep, observed, w_in, b_in.reshape(1, units), w_out, b_out.reshape(1, width))

    swap = [(i, i ^ 1) for i in range(size)]
    early = lax.ppermute(last, "tm", swap)
    row = start.reshape(1, width)
    entry = jnp.where(position == 1, row, 0.0)
    chip, leaving = pl.pallas_call(
        pair_kernel,
        out_shape=(shape((width + 8, width), F32), shape((1, width), F32)),
        in_specs=[VMEM] * 3,
        out_specs=(VMEM,) * 2,
        compiler_params=params(),
    )(early, last, entry)
    for chip_at in range(1, size // 2):
        moved = lax.ppermute(leaving, "tm", [(2 * chip_at - 1, 2 * chip_at + 1)])
        entry = entry + moved
        if chip_at < size // 2 - 1:
            leaving = pl.pallas_call(
                hop_kernel,
                out_shape=shape((1, width), F32),
                in_specs=[VMEM] * 2,
                out_specs=VMEM,
                compiler_params=params(),
            )(chip, entry)
    other = lax.ppermute(entry, "tm", swap)
    late = jnp.broadcast_to((position % 2).astype(F32), (1, width))
    return pl.pallas_call(
        final_kernel,
        out_shape=shape((n_steps, width), F32),
        in_specs=[VMEM] * 7,
        out_specs=VMEM,
        compiler_params=params(),
    )(early, pre, last, offsets, entry, other, late)


def solution(mesh):
    rows = P(("groups", "tm"), None)
    placed = (rows, rows, rows, rows, P("groups"), P(), P(), P(), P())
    return jax.shard_map(body, mesh=mesh, in_specs=placed, out_specs=rows, check_vma=False)
```

```python
import functools
import math

import jax
import jax.numpy as jnp
from jax import lax
from jax.experimental import pallas as pl
from jax.experimental.pallas import tpu as pltpu
from jax.sharding import PartitionSpec as P

C0 = math.sqrt(2.0 / math.pi)
C1 = 0.044715 * C0
LANES = 128
F32 = jnp.float32
BF16 = jnp.bfloat16
VMEM = pl.BlockSpec(memory_space=pltpu.VMEM)
HBM = pl.BlockSpec(memory_space=pltpu.HBM)


def split(x):
    hi = x.astype(BF16)
    return hi, (x - hi.astype(F32)).astype(BF16)


def product(left, right):
    lhi, llo = split(left)
    rhi, rlo = split(right)
    return jnp.dot(
        jnp.concatenate([lhi, llo, lhi], axis=1),
        jnp.concatenate([rhi, rhi, rlo], axis=0),
        preferred_element_type=F32,
    )


def columns_of(row):
    width = row.shape[1]
    return [
        jnp.transpose(jnp.broadcast_to(row[:, b : b + LANES], (LANES, LANES)))
        for b in range(0, width, LANES)
    ]


def row_times(cols, matrix):
    width = len(cols) * LANES
    parts = []
    for c in range(0, width, LANES):
        total = None
        for b in range(len(cols)):
            term = jnp.sum(
                (cols[b] * matrix(pl.ds(b * LANES, LANES), pl.ds(c, LANES))).reshape(LANES // 8, 8, LANES),
                axis=0,
            )
            total = term if total is None else total + term
        parts.append(jnp.sum(total, axis=0, keepdims=True))
    return jnp.concatenate(parts, axis=1)


def net_kernel(
    mean_h, spread_h, keep_h, obs_h, b_in_h, b_out_h, w_in_h, w_out_h,
    pre, last, offsets,
    mean_ref, spread_ref, keep_ref, obs_ref, b_in, b_out, w_in, w_out,
    turned, w_wide, base, wide, h0, h1, jac, pm, held_ref, sems, out_sems,
):
    n_steps, width = mean_ref.shape
    units = w_in.shape[1]
    half = width // 2
    factor = math.sqrt(width + 1.0)
    sources = (mean_h, spread_h, keep_h, obs_h, b_in_h, b_out_h)
    targets = (mean_ref, spread_ref, keep_ref, obs_ref, b_in, b_out)
    copies = [
        pltpu.make_async_copy(source, target, sems.at[i])
        for i, (source, target) in enumerate(zip(sources, targets))
    ]
    quarter = units // 4
    for i in range(4):
        part = pl.ds(i * quarter, quarter)
        copies.append(pltpu.make_async_copy(w_in_h.at[:, part], w_in.at[:, part], sems.at[6 + i]))
    copies.append(pltpu.make_async_copy(w_out_h, w_out, sems.at[10]))
    for copy in copies:
        copy.start()
    for copy in copies[:6]:
        copy.wait()

    mean = mean_ref[...]
    centre_pts = mean.astype(BF16)
    centre_f = centre_pts.astype(F32)
    spread = spread_ref[...]
    up = (mean + factor * spread).astype(BF16).astype(F32)
    lo = (mean - factor * spread).astype(BF16).astype(F32)
    inv = 1.0 / (2.0 * factor * spread)
    eye = lax.broadcasted_iota(jnp.int32, (LANES, LANES), 0) == lax.broadcasted_iota(
        jnp.int32, (LANES, LANES), 1
    )
    kinds = (0.5 * (up - centre_f), 0.5 * (lo - centre_f), inv, (up - lo) * inv)
    stacked = jnp.concatenate(kinds + (jnp.zeros((LANES - 4 * n_steps, width), F32),), axis=0)
    for b in range(0, width, LANES):
        turned[pl.ds(b, LANES), :] = jnp.transpose(stacked[:, b : b + LANES])

    def widen(k):
        for b in range(0, width, LANES):
            for a in range(4):
                at = a * n_steps + k
                block = jnp.broadcast_to(turned[pl.ds(b, LANES), at : at + 1], (LANES, LANES))
                if a == 3:
                    block = jnp.where(eye, block, 0.0)
                wide[a, k, pl.ds(b, LANES), :] = block

    widen(0)

    def gelu(k, j0, dst):
        for c in range(0, units, 256):
            if k == 0 and j0 == 0 and c % quarter == 0:
                copies[6 + c // quarter].wait()
                part = pl.ds(c, quarter)
                base[:, part] = (
                    jnp.dot(centre_pts, w_in[:, part], preferred_element_type=F32) + b_in[:, part]
                ) * 0.5
            b = base[pl.ds(k, 1), pl.ds(c, 256)]
            for r in range(0, half, 16):
                place = (pl.ds(j0 + r, 16), pl.ds(c, 256))
                if k == 0:
                    w = w_in[place].astype(F32)
                    w_wide[place] = w
                else:
                    w = w_wide[place]
                for s in range(2):
                    d = wide[s, k, pl.ds(j0 + r, 16), :]
                    y = b + jnp.concatenate([d, d], axis=1) * w
                    z = y * (y * y * (8.0 * C1) + 2.0 * C0)
                    dst[pl.ds(s * half + r, 16), pl.ds(c, 256)] = (y * jnp.tanh(z) + y).astype(BF16)

    def outer(k, j0, src):
        out = jnp.dot(src[...], w_out[...], preferred_element_type=F32)
        keep = keep_ref[pl.ds(k, 1), :]
        sums = []
        for c in range(0, width, LANES):
            upper, lower = out[:half, c : c + LANES], out[half:, c : c + LANES]
            for r in range(0, half, LANES):
                v = (upper[r : r + LANES] - lower[r : r + LANES]) * wide[2, k, pl.ds(j0 + r, LANES), :]
                if c == j0 + r:
                    v = v + wide[3, k, pl.ds(c, LANES), :]
                jac[k, pl.ds(j0 + r, LANES), pl.ds(c, LANES)] = v * keep[:, c : c + LANES]
            sums.append(jnp.sum(upper + lower, axis=0, keepdims=True))
        return jnp.concatenate(sums, axis=1)

    sends = []

    def compose(k):
        held = product(held_ref[k - 1] if k > 1 else jac[0], jac[k])
        if k < n_steps - 1:
            held_ref[k] = held
        else:
            last[pl.ds(0, width), :] = held
        if k < n_steps - 1:
            sends.append(pltpu.make_async_copy(held_ref.at[k], pre.at[k], out_sems.at[k]))
            sends[-1].start()

    slots = (h0, h1)
    tiles = 2 * n_steps
    for tile in range(tiles + 1):
        if tile < tiles:
            gelu(tile // 2, (tile % 2) * half, slots[tile % 2])
        if tile % 2 == 0 and tile + 2 < tiles:
            widen(tile // 2 + 1)
        if tile == 0:
            copies[10].wait()
        if tile > 0:
            k, side = (tile - 1) // 2, (tile - 1) % 2
            total = outer(k, side * half, slots[side])
            pm[pl.ds(k, 1), :] = total if side == 0 else pm[pl.ds(k, 1), :] + total
        if tile == 3:
            sends.append(pltpu.make_async_copy(jac.at[0], pre.at[0], out_sems.at[0]))
            sends[-1].start()
        if tile >= 5 and tile % 2 == 1:
            compose((tile - 3) // 2)

    points = 2.0 * width
    y = base[...]
    z = y * (y * y * (8.0 * C1) + 2.0 * C0)
    hidden = (y * jnp.tanh(z) + y).astype(BF16)
    centre = jnp.dot(hidden, w_out[...], preferred_element_type=F32) + b_out[...] + centre_f
    sums = pm[pl.ds(0, n_steps), :] + points * b_out[...] + ((points - 2.0) * centre_f + (up + lo))
    point_mean = centre / (width + 1.0) + sums / (2.0 * (width + 1.0))
    keep = keep_ref[...]
    free = keep * point_mean + (1.0 - keep) * obs_ref[...]
    consts = []
    for k in range(n_steps):
        moved = row_times(columns_of(mean[k : k + 1]), lambda r, c: jac[k, r, c])
        consts.append(free[k : k + 1] - moved)

    for k in range((tiles - 3) // 2 + 1, n_steps):
        compose(k)
    const = consts[0]
    offsets[pl.ds(0, 1), :] = const
    for k in range(1, n_steps):
        const = row_times(columns_of(const), lambda r, c: jac[k, r, c]) + consts[k]
        offsets[pl.ds(k, 1), :] = const
    last[pl.ds(width, 8), :] = jnp.concatenate([const, jnp.zeros((7, width), F32)], axis=0)
    for send in sends:
        send.wait()


def fetch_kernel(source, target, sem):
    copy = pltpu.make_async_copy(source, target, sem)
    copy.start()
    copy.wait()


def first_kernel(early, late, entry, leaving):
    width = late.shape[1]
    mid = row_times(columns_of(entry[...]), lambda r, c: early[r, c]) + early[pl.ds(width, 1), :]
    leaving[...] = row_times(columns_of(mid), lambda r, c: late[r, c]) + late[pl.ds(width, 1), :]


def pair_kernel(early, late, chip):
    width = late.shape[1]
    both = product(early[...], late[pl.ds(0, width), :])
    chip[pl.ds(0, width), :] = both[:width]
    const = both[width : width + 1] + late[pl.ds(width, 1), :]
    chip[pl.ds(width, 8), :] = jnp.broadcast_to(const, (8, width))


def hop_kernel(chip, entry, leaving):
    width = chip.shape[1]
    leaving[...] = row_times(columns_of(entry[...]), lambda r, c: chip[r, c]) + chip[pl.ds(width, 1), :]


def final_kernel(early, pre_h, last, offsets_h, entry, other, late_mask, out, pre, offsets, sems):
    n_steps, width = offsets.shape
    gets = [pltpu.make_async_copy(pre_h.at[k], pre.at[k], sems.at[k]) for k in range(n_steps - 1)]
    gets.append(pltpu.make_async_copy(offsets_h, offsets, sems.at[n_steps - 1]))
    for get in gets:
        get.start()
    mid = row_times(columns_of(entry[...]), lambda r, c: early[r, c]) + early[pl.ds(width, 1), :]
    begin = jnp.where(late_mask[...] > 0.0, mid, other[...])
    cols = columns_of(begin)
    gets[n_steps - 1].wait()
    for k in range(n_steps):
        if k < n_steps - 1:
            gets[k].wait()
            moved = row_times(cols, lambda r, c: pre[k, r, c])
        else:
            moved = row_times(cols, lambda r, c: last[r, c])
        out[pl.ds(k, 1), :] = moved + offsets[pl.ds(k, 1), :]


def params(mib):
    return pltpu.CompilerParams(vmem_limit_bytes=mib * 1024 * 1024)


def body(lin_mean, spread, keep, observed, start, w_in, b_in, w_out, b_out):
    n_steps, width = lin_mean.shape
    units = w_in.shape[1]
    size = lax.axis_size("tm")
    position = lax.axis_index("tm")
    shape = jax.ShapeDtypeStruct

    small = pltpu.VMEM((n_steps, width), F32)
    pre, last, offsets = pl.pallas_call(
        net_kernel,
        out_shape=(
            shape((n_steps - 1, width, width), F32),
            shape((width + 8, width), F32),
            shape((n_steps, width), F32),
        ),
        in_specs=[HBM] * 8,
        out_specs=(HBM, VMEM, VMEM),
        scratch_shapes=[
            small, small, small, small,
            pltpu.VMEM((1, units), F32),
            pltpu.VMEM((1, width), F32),
            pltpu.VMEM((width, units), BF16),
            pltpu.VMEM((units, width), BF16),
            pltpu.VMEM((width, LANES), F32),
            pltpu.VMEM((width, units), F32),
            pltpu.VMEM((n_steps, units), F32),
            pltpu.VMEM((4, n_steps, width, LANES), F32),
            pltpu.VMEM((width, units), BF16),
            pltpu.VMEM((width, units), BF16),
            pltpu.VMEM((n_steps, width, width), F32),
            pltpu.VMEM((8, width), F32),
            pltpu.VMEM((n_steps - 1, width, width), F32),
            pltpu.SemaphoreType.DMA((11,)),
            pltpu.SemaphoreType.DMA((n_steps,)),
        ],
        compiler_params=params(60),
    )(lin_mean, spread, keep, observed, b_in.reshape(1, units), b_out.reshape(1, width), w_in, w_out)

    swap = [(i, i ^ 1) for i in range(size)]
    row = start.reshape(1, width)
    early = lax.ppermute(last, "tm", swap)
    late = pl.pallas_call(
        fetch_kernel,
        out_shape=shape((width + 8, width), F32),
        in_specs=[HBM],
        out_specs=VMEM,
        scratch_shapes=[pltpu.SemaphoreType.DMA],
        compiler_params=params(16),
    )(last)
    leaving = pl.pallas_call(
        first_kernel,
        out_shape=shape((1, width), F32),
        in_specs=[VMEM] * 3,
        out_specs=VMEM,
        compiler_params=params(16),
    )(early, late, row)
    chip = pl.pallas_call(
        pair_kernel,
        out_shape=shape((width + 8, width), F32),
        in_specs=[VMEM] * 2,
        out_specs=VMEM,
        compiler_params=params(16),
    )(early, late)
    entry = row
    for chip_at in range(1, size // 2):
        if chip_at % 2 == 1 and size % 4 == 0:
            moved = lax.ppermute(leaving, "tm", [(i, i ^ 2) for i in range(size)])
        else:
            moved = lax.ppermute(leaving, "tm", [(2 * chip_at - 1, 2 * chip_at + 1)])
        entry = jnp.where(position == 2 * chip_at + 1, moved, entry)
        if chip_at < size // 2 - 1:
            leaving = pl.pallas_call(
                hop_kernel,
                out_shape=shape((1, width), F32),
                in_specs=[VMEM] * 2,
                out_specs=VMEM,
                compiler_params=params(16),
            )(chip, entry)
    other = lax.ppermute(entry, "tm", swap)
    late_mask = jnp.broadcast_to((position % 2).astype(F32), (1, width))
    return pl.pallas_call(
        final_kernel,
        out_shape=shape((n_steps, width), F32),
        in_specs=[VMEM, HBM, VMEM, HBM] + [VMEM] * 3,
        out_specs=VMEM,
        scratch_shapes=[
            pltpu.VMEM((n_steps - 1, width, width), F32),
            pltpu.VMEM((n_steps, width), F32),
            pltpu.SemaphoreType.DMA((n_steps,)),
        ],
        compiler_params=params(50),
    )(early, pre, late, offsets, entry, other, late_mask)


def solution(mesh):
    rows = P(("groups", "tm"), None)
    placed = (rows, rows, rows, rows, P("groups"), P(), P(), P(), P())
    return jax.shard_map(body, mesh=mesh, in_specs=placed, out_specs=rows, check_vma=False)
```

```python
import functools
import math

import jax
import jax.numpy as jnp
from jax import lax
from jax.experimental import pallas as pl
from jax.experimental.pallas import tpu as pltpu
from jax.sharding import PartitionSpec as P

C0 = math.sqrt(2.0 / math.pi)
C1 = 0.044715 * C0
LANES = 128
F32 = jnp.float32
BF16 = jnp.bfloat16
VMEM = pl.BlockSpec(memory_space=pltpu.VMEM)
HBM = pl.BlockSpec(memory_space=pltpu.HBM)


def split(x):
    hi = x.astype(BF16)
    return hi, (x - hi.astype(F32)).astype(BF16)


def product(left, right):
    lhi, llo = split(left)
    rhi, rlo = split(right)
    both = jnp.dot(jnp.concatenate([lhi, llo], axis=0), rhi, preferred_element_type=F32)
    rows = left.shape[0]
    return both[:rows] + both[rows:] + jnp.dot(lhi, rlo, preferred_element_type=F32)


def columns_of(row):
    width = row.shape[1]
    return [
        jnp.transpose(jnp.broadcast_to(row[:, b : b + LANES], (LANES, LANES)))
        for b in range(0, width, LANES)
    ]


def row_times(cols, matrix):
    width = len(cols) * LANES
    parts = []
    for c in range(0, width, LANES):
        total = None
        for b in range(len(cols)):
            term = jnp.sum(
                (cols[b] * matrix(pl.ds(b * LANES, LANES), pl.ds(c, LANES))).reshape(LANES // 8, 8, LANES),
                axis=0,
            )
            total = term if total is None else total + term
        parts.append(jnp.sum(total, axis=0, keepdims=True))
    return jnp.concatenate(parts, axis=1)


def net_kernel(
    mean_h, spread_h, keep_h, obs_h, b_in_h, b_out_h, w_in_h, w_out_h,
    steps, last, free,
    mean_ref, spread_ref, keep_ref, obs_ref, b_in, b_out, w_in, w_out,
    turned, w_wide, base, wide, h0, h1, jac, pm, known_ref, held_ref, sems, out_sems,
):
    n_steps, width = mean_ref.shape
    units = w_in.shape[1]
    half = width // 2
    factor = math.sqrt(width + 1.0)
    sources = (mean_h, spread_h, keep_h, obs_h, b_in_h, b_out_h)
    targets = (mean_ref, spread_ref, keep_ref, obs_ref, b_in, b_out)
    copies = [
        pltpu.make_async_copy(source, target, sems.at[i])
        for i, (source, target) in enumerate(zip(sources, targets))
    ]
    quarter = units // 4
    for i in range(4):
        part = pl.ds(i * quarter, quarter)
        copies.append(pltpu.make_async_copy(w_in_h.at[:, part], w_in.at[:, part], sems.at[6 + i]))
    copies.append(pltpu.make_async_copy(w_out_h, w_out, sems.at[10]))
    for copy in copies:
        copy.start()
    for copy in copies[:6]:
        copy.wait()


    mean = mean_ref[...]
    centre_pts = mean.astype(BF16)
    centre_f = centre_pts.astype(F32)
    spread = spread_ref[...]
    up = (mean + factor * spread).astype(BF16).astype(F32)
    lo = (mean - factor * spread).astype(BF16).astype(F32)
    inv = 1.0 / (2.0 * factor * spread)
    eye = lax.broadcasted_iota(jnp.int32, (LANES, LANES), 0) == lax.broadcasted_iota(
        jnp.int32, (LANES, LANES), 1
    )
    kinds = (0.5 * (up - centre_f), 0.5 * (lo - centre_f), inv, (up - lo) * inv)
    stacked = jnp.concatenate(kinds + (jnp.zeros((LANES - 4 * n_steps, width), F32),), axis=0)
    for b in range(0, width, LANES):
        turned[pl.ds(b, LANES), :] = jnp.transpose(stacked[:, b : b + LANES])

    def widen(k, kinds):
        for b in range(0, width, LANES):
            for a in kinds:
                at = a * n_steps + k
                block = jnp.broadcast_to(turned[pl.ds(b, LANES), at : at + 1], (LANES, LANES))
                if a == 3:
                    block = jnp.where(eye, block, 0.0)
                wide[a, k, pl.ds(b, LANES), :] = block

    widen(0, (0, 1))

    def gelu(k, j0, dst):
        for c in range(0, units, 256):
            if k == 0 and j0 == 0 and c == 3 * quarter:
                copies[10].wait()
            if k == 0 and j0 == 0 and c % quarter == 0:
                copies[6 + c // quarter].wait()
                part = pl.ds(c, quarter)
                base[:, part] = (
                    jnp.dot(centre_pts, w_in[:, part], preferred_element_type=F32) + b_in[:, part]
                ) * 0.5
            b = base[pl.ds(k, 1), pl.ds(c, 256)]
            for r in range(0, half, 16):
                place = (pl.ds(j0 + r, 16), pl.ds(c, 256))
                if k == 0:
                    w = w_in[place].astype(F32)
                    w_wide[place] = w
                else:
                    w = w_wide[place]
                for s in range(2):
                    d = wide[s, k, pl.ds(j0 + r, 16), :]
                    y = b + jnp.concatenate([d, d], axis=1) * w
                    z = y * (y * y * (8.0 * C1) + 2.0 * C0)
                    dst[pl.ds(s * half + r, 16), pl.ds(c, 256)] = (y * jnp.tanh(z) + y).astype(BF16)

    def outer(k, j0, src):
        out = jnp.dot(src[...], w_out[...], preferred_element_type=F32)
        keep = keep_ref[pl.ds(k, 1), :]
        sums = []
        for c in range(0, width, LANES):
            upper, lower = out[:half, c : c + LANES], out[half:, c : c + LANES]
            for r in range(0, half, LANES):
                v = (upper[r : r + LANES] - lower[r : r + LANES]) * wide[2, k, pl.ds(j0 + r, LANES), :]
                if c == j0 + r:
                    v = v + wide[3, k, pl.ds(c, LANES), :]
                jac[k, pl.ds(j0 + r, LANES), pl.ds(c, LANES)] = v * keep[:, c : c + LANES]
            sums.append(jnp.sum(upper + lower, axis=0, keepdims=True))
        return jnp.concatenate(sums, axis=1)

    sends = []

    def compose(k):
        held = product(held_ref[k - 1] if k > 1 else jac[0], jac[k])
        if k < n_steps - 1:
            held_ref[k] = held
        else:
            last[pl.ds(0, width), :] = held

    points = 2.0 * width
    slots = (h0, h1)
    tiles = 2 * n_steps
    for tile in range(tiles + 1):
        if tile == tiles - 1:
            for k in range(n_steps - 1):
                sends.append(pltpu.make_async_copy(jac.at[k], steps.at[k], out_sems.at[k]))
                sends[-1].start()
        if tile > 0:
            k, side = (tile - 1) // 2, (tile - 1) % 2
            total = outer(k, side * half, slots[side])
            pm[pl.ds(k, 1), :] = total if side == 0 else pm[pl.ds(k, 1), :] + total
        if tile >= 5 and tile % 2 == 1:
            compose((tile - 3) // 2)
        if tile < tiles:
            gelu(tile // 2, (tile % 2) * half, slots[tile % 2])
        if tile == 0:
            widen(0, (2, 3))
        if tile == 2:
            y = base[...]
            z = y * (y * y * (8.0 * C1) + 2.0 * C0)
            hidden = (y * jnp.tanh(z) + y).astype(BF16)
            centre = jnp.dot(hidden, w_out[...], preferred_element_type=F32) + b_out[...] + centre_f
            keep = keep_ref[...]
            known = keep * (
                centre / (width + 1.0)
                + (points * b_out[...] + ((points - 2.0) * centre_f + (up + lo))) / (2.0 * (width + 1.0))
            ) + (1.0 - keep) * obs_ref[...]
            known_ref[pl.ds(0, n_steps), :] = known
        if tile % 2 == 0 and tile + 2 < tiles:
            widen(tile // 2 + 1, (0, 1, 2, 3))
    for k in range((tiles - 3) // 2 + 1, n_steps):
        compose(k)
    const = jnp.zeros((1, width), F32)
    for k in range(n_steps):
        row = pl.ds(k, 1)
        own = known_ref[row, :] + keep_ref[row, :] * (pm[row, :] / (2.0 * (width + 1.0)))
        free[row, :] = own
        const = row_times(columns_of(const - mean_ref[row, :]), lambda r, c: jac[k, r, c]) + own
    last[pl.ds(width, 8), :] = jnp.concatenate([const, jnp.zeros((7, width), F32)], axis=0)
    for send in sends:
        send.wait()


def fetch_kernel(count, *refs):
    sources, targets, sems = refs[:count], refs[-1 - count : -1], refs[-1]
    copies = [
        pltpu.make_async_copy(source, target, sems.at[i])
        for i, (source, target) in enumerate(zip(sources, targets))
    ]
    for copy in copies:
        copy.start()
    for copy in copies:
        copy.wait()


def fetch(arrays, after=()):
    return pl.pallas_call(
        functools.partial(fetch_kernel, len(arrays)),
        out_shape=tuple(jax.ShapeDtypeStruct(x.shape, x.dtype) for x in arrays),
        in_specs=[HBM] * len(arrays) + [VMEM] * len(after),
        out_specs=(VMEM,) * len(arrays),
        scratch_shapes=[pltpu.SemaphoreType.DMA((len(arrays),))],
        compiler_params=params(16),
    )(*arrays, *after)


def first_kernel(early, late, entry, leaving):
    width = late.shape[1]
    mid = row_times(columns_of(entry[...]), lambda r, c: early[r, c]) + early[pl.ds(width, 1), :]
    leaving[...] = row_times(columns_of(mid), lambda r, c: late[r, c]) + late[pl.ds(width, 1), :]


def pair_kernel(early, late, chip):
    width = late.shape[1]
    both = product(early[...], late[pl.ds(0, width), :])
    chip[pl.ds(0, width), :] = both[:width]
    const = both[width : width + 1] + late[pl.ds(width, 1), :]
    chip[pl.ds(width, 8), :] = jnp.broadcast_to(const, (8, width))


def hop_kernel(chip_at, chip, held, moved, *refs):
    entry, leaving = refs[-2:]
    width = chip.shape[1]
    arrived = lax.axis_index("tm") == 2 * chip_at + 1
    row = jnp.where(arrived, moved[...], held[...])
    entry[...] = row
    leaving[...] = row_times(columns_of(row), lambda r, c: chip[r, c]) + chip[pl.ds(width, 1), :]


def arrive_kernel(chip_at, held, moved, entry):
    entry[...] = jnp.where(lax.axis_index("tm") == 2 * chip_at + 1, moved[...], held[...])


def final_kernel(early, steps, last, free, mean, entry, other, out):
    n_steps, width = free.shape
    mid = row_times(columns_of(entry[...]), lambda r, c: early[r, c]) + early[pl.ds(width, 1), :]
    state = jnp.where(lax.axis_index("tm") % 2 == 1, mid, other[...])
    out[pl.ds(n_steps - 1, 1), :] = (
        row_times(columns_of(state), lambda r, c: last[r, c]) + last[pl.ds(width, 1), :]
    )
    for k in range(n_steps - 1):
        row = pl.ds(k, 1)
        state = row_times(columns_of(state - mean[row, :]), lambda r, c: steps[k, r, c]) + free[row, :]
        out[row, :] = state


def params(mib):
    return pltpu.CompilerParams(vmem_limit_bytes=mib * 1024 * 1024)


def body(lin_mean, spread, keep, observed, start, w_in, b_in, w_out, b_out):
    n_steps, width = lin_mean.shape
    units = w_in.shape[1]
    size = lax.axis_size("tm")
    shape = jax.ShapeDtypeStruct

    small = pltpu.VMEM((n_steps, width), F32)
    steps, last, free = pl.pallas_call(
        net_kernel,
        out_shape=(
            shape((n_steps - 1, width, width), F32),
            shape((width + 8, width), F32),
            shape((n_steps, width), F32),
        ),
        in_specs=[HBM] * 8,
        out_specs=(HBM, VMEM, VMEM),
        scratch_shapes=[
            small, small, small, small,
            pltpu.VMEM((1, units), F32),
            pltpu.VMEM((1, width), F32),
            pltpu.VMEM((width, units), BF16),
            pltpu.VMEM((units, width), BF16),
            pltpu.VMEM((width, LANES), F32),
            pltpu.VMEM((width, units), F32),
            pltpu.VMEM((n_steps, units), F32),
            pltpu.VMEM((4, n_steps, width, LANES), F32),
            pltpu.VMEM((width, units), BF16),
            pltpu.VMEM((width, units), BF16),
            pltpu.VMEM((n_steps, width, width), F32),
            pltpu.VMEM((8, width), F32),
            pltpu.VMEM((8, width), F32),
            pltpu.VMEM((n_steps - 1, width, width), F32),
            pltpu.SemaphoreType.DMA((11,)),
            pltpu.SemaphoreType.DMA((n_steps,)),
        ],
        compiler_params=params(60),
    )(lin_mean, spread, keep, observed, b_in.reshape(1, units), b_out.reshape(1, width), w_in, w_out)

    swap = [(i, i ^ 1) for i in range(size)]
    row = start.reshape(1, width)
    early = lax.ppermute(last, "tm", swap)
    (late,) = fetch((last,))
    leaving = pl.pallas_call(
        first_kernel,
        out_shape=shape((1, width), F32),
        in_specs=[VMEM] * 3,
        out_specs=VMEM,
        compiler_params=params(16),
    )(early, late, row)
    chip = pl.pallas_call(
        pair_kernel,
        out_shape=shape((width + 8, width), F32),
        in_specs=[VMEM] * 2,
        out_specs=VMEM,
        compiler_params=params(16),
    )(early, late)
    row_shape = shape((1, width), F32)
    entry = row
    for chip_at in range(1, size // 2):
        if chip_at % 2 == 1 and size % 4 == 0:
            moved = lax.ppermute(leaving, "tm", [(i, i ^ 2) for i in range(size)])
        else:
            moved = lax.ppermute(leaving, "tm", [(2 * chip_at - 1, 2 * chip_at + 1)])
        ready = (free,) if chip_at == 2 else ()
        if chip_at == 1:
            steps, free, lin_mean = fetch((steps, free, lin_mean), (moved,))
        if chip_at < size // 2 - 1:
            entry, leaving = pl.pallas_call(
                functools.partial(hop_kernel, chip_at),
                out_shape=(row_shape, row_shape),
                in_specs=[VMEM] * (3 + len(ready)),
                out_specs=(VMEM, VMEM),
                compiler_params=params(16),
            )(chip, entry, moved, *ready)
        else:
            entry = pl.pallas_call(
                functools.partial(arrive_kernel, chip_at),
                out_shape=row_shape,
                in_specs=[VMEM] * 2,
                out_specs=VMEM,
                compiler_params=params(16),
            )(entry, moved)
    other = lax.ppermute(entry, "tm", swap)
    return pl.pallas_call(
        final_kernel,
        out_shape=shape((n_steps, width), F32),
        in_specs=[VMEM] * 7,
        out_specs=VMEM,
        compiler_params=params(16),
    )(early, steps, late, free, lin_mean, entry, other)


def solution(mesh):
    rows = P(("groups", "tm"), None)
    placed = (rows, rows, rows, rows, P("groups"), P(), P(), P(), P())
    return jax.shard_map(body, mesh=mesh, in_specs=placed, out_specs=rows, check_vma=False)
```

```python
import functools
import math

import jax
import jax.numpy as jnp
from jax import lax
from jax.experimental import pallas as pl
from jax.experimental.pallas import tpu as pltpu
from jax.sharding import PartitionSpec as P

C0 = math.sqrt(2.0 / math.pi)
C1 = 0.044715 * C0
LANES = 128
F32 = jnp.float32
BF16 = jnp.bfloat16
VMEM = pl.BlockSpec(memory_space=pltpu.VMEM)
HBM = pl.BlockSpec(memory_space=pltpu.HBM)


def split(x):
    hi = x.astype(BF16)
    return hi, (x - hi.astype(F32)).astype(BF16)


def product(left, right):
    lhi, llo = split(left)
    rhi, rlo = split(right)
    both = jnp.dot(jnp.concatenate([lhi, llo], axis=0), rhi, preferred_element_type=F32)
    rows = left.shape[0]
    return both[:rows] + both[rows:] + jnp.dot(lhi, rlo, preferred_element_type=F32)


def columns_of(row):
    width = row.shape[1]
    return [
        jnp.transpose(jnp.broadcast_to(row[:, b : b + LANES], (LANES, LANES)))
        for b in range(0, width, LANES)
    ]


def row_times(cols, matrix):
    width = len(cols) * LANES
    parts = []
    for c in range(0, width, LANES):
        total = None
        for b in range(len(cols)):
            term = jnp.sum(
                (cols[b] * matrix(pl.ds(b * LANES, LANES), pl.ds(c, LANES))).reshape(LANES // 8, 8, LANES),
                axis=0,
            )
            total = term if total is None else total + term
        parts.append(jnp.sum(total, axis=0, keepdims=True))
    return jnp.concatenate(parts, axis=1)


def net_kernel(
    mean_h, spread_h, keep_h, obs_h, b_in_h, b_out_h, start_h, w_in_h, w_out_h,
    steps, last, free, first,
    mean_ref, spread_ref, keep_ref, obs_ref, b_in, b_out, start, w_in, w_out,
    turned, w_wide, base, wide, h0, h1, jac, pm, known_ref, held_ref, sems, out_sems,
):
    n_steps, width = mean_ref.shape
    units = w_in.shape[1]
    half = width // 2
    factor = math.sqrt(width + 1.0)
    sources = (mean_h, spread_h, keep_h, obs_h, b_in_h, b_out_h, start_h)
    targets = (mean_ref, spread_ref, keep_ref, obs_ref, b_in, b_out, start)
    copies = [
        pltpu.make_async_copy(source, target, sems.at[i])
        for i, (source, target) in enumerate(zip(sources, targets))
    ]
    quarter = units // 4
    for i in range(4):
        part = pl.ds(i * quarter, quarter)
        copies.append(pltpu.make_async_copy(w_in_h.at[:, part], w_in.at[:, part], sems.at[7 + i]))
    copies.append(pltpu.make_async_copy(w_out_h, w_out, sems.at[11]))
    for copy in copies:
        copy.start()
    for copy in copies[:7]:
        copy.wait()


    mean = mean_ref[...]
    centre_pts = mean.astype(BF16)
    centre_f = centre_pts.astype(F32)
    spread = spread_ref[...]
    up = (mean + factor * spread).astype(BF16).astype(F32)
    lo = (mean - factor * spread).astype(BF16).astype(F32)
    inv = 1.0 / (2.0 * factor * spread)
    eye = lax.broadcasted_iota(jnp.int32, (LANES, LANES), 0) == lax.broadcasted_iota(
        jnp.int32, (LANES, LANES), 1
    )
    kinds = (0.5 * (up - centre_f), 0.5 * (lo - centre_f), inv, (up - lo) * inv)
    stacked = jnp.concatenate(kinds + (jnp.zeros((LANES - 4 * n_steps, width), F32),), axis=0)
    for b in range(0, width, LANES):
        turned[pl.ds(b, LANES), :] = jnp.transpose(stacked[:, b : b + LANES])

    def widen(k, kinds):
        for b in range(0, width, LANES):
            for a in kinds:
                at = a * n_steps + k
                block = jnp.broadcast_to(turned[pl.ds(b, LANES), at : at + 1], (LANES, LANES))
                if a == 3:
                    block = jnp.where(eye, block, 0.0)
                wide[a, k, pl.ds(b, LANES), :] = block

    widen(0, (0, 1))

    def gelu(k, j0, dst):
        for c in range(0, units, 256):
            if k == 0 and j0 == 0 and c == 3 * quarter:
                copies[11].wait()
            if k == 0 and j0 == 0 and c % quarter == 0:
                copies[7 + c // quarter].wait()
                part = pl.ds(c, quarter)
                base[:, part] = (
                    jnp.dot(centre_pts, w_in[:, part], preferred_element_type=F32) + b_in[:, part]
                ) * 0.5
            b = base[pl.ds(k, 1), pl.ds(c, 256)]
            for r in range(0, half, 16):
                place = (pl.ds(j0 + r, 16), pl.ds(c, 256))
                if k == 0:
                    w = w_in[place].astype(F32)
                    w_wide[place] = w
                else:
                    w = w_wide[place]
                for s in range(2):
                    d = wide[s, k, pl.ds(j0 + r, 16), :]
                    y = b + jnp.concatenate([d, d], axis=1) * w
                    z = y * (y * y * (8.0 * C1) + 2.0 * C0)
                    dst[pl.ds(s * half + r, 16), pl.ds(c, 256)] = (y * jnp.tanh(z) + y).astype(BF16)

    def outer(k, j0, src):
        out = jnp.dot(src[...], w_out[...], preferred_element_type=F32)
        keep = keep_ref[pl.ds(k, 1), :]
        sums = []
        for c in range(0, width, LANES):
            upper, lower = out[:half, c : c + LANES], out[half:, c : c + LANES]
            for r in range(0, half, LANES):
                v = (upper[r : r + LANES] - lower[r : r + LANES]) * wide[2, k, pl.ds(j0 + r, LANES), :]
                if c == j0 + r:
                    v = v + wide[3, k, pl.ds(c, LANES), :]
                jac[k, pl.ds(j0 + r, LANES), pl.ds(c, LANES)] = v * keep[:, c : c + LANES]
            sums.append(jnp.sum(upper + lower, axis=0, keepdims=True))
        return jnp.concatenate(sums, axis=1)

    sends = []

    def compose(k):
        held = product(held_ref[k - 1] if k > 1 else jac[0], jac[k])
        if k < n_steps - 1:
            held_ref[k] = held
        else:
            last[pl.ds(0, width), :] = held

    points = 2.0 * width
    slots = (h0, h1)
    tiles = 2 * n_steps
    for tile in range(tiles + 1):
        if tile == tiles - 1:
            for k in range(n_steps - 1):
                sends.append(pltpu.make_async_copy(jac.at[k], steps.at[k], out_sems.at[k]))
                sends[-1].start()
        if tile > 0:
            k, side = (tile - 1) // 2, (tile - 1) % 2
            total = outer(k, side * half, slots[side])
            pm[pl.ds(k, 1), :] = total if side == 0 else pm[pl.ds(k, 1), :] + total
        if tile >= 5 and tile % 2 == 1:
            compose((tile - 3) // 2)
        if tile < tiles:
            gelu(tile // 2, (tile % 2) * half, slots[tile % 2])
        if tile == 0:
            widen(0, (2, 3))
        if tile == 2:
            y = base[...]
            z = y * (y * y * (8.0 * C1) + 2.0 * C0)
            hidden = (y * jnp.tanh(z) + y).astype(BF16)
            centre = jnp.dot(hidden, w_out[...], preferred_element_type=F32) + b_out[...] + centre_f
            keep = keep_ref[...]
            known = keep * (
                centre / (width + 1.0)
                + (points * b_out[...] + ((points - 2.0) * centre_f + (up + lo))) / (2.0 * (width + 1.0))
            ) + (1.0 - keep) * obs_ref[...]
            known_ref[pl.ds(0, n_steps), :] = known
        if tile % 2 == 0 and tile + 2 < tiles:
            widen(tile // 2 + 1, (0, 1, 2, 3))
    for k in range((tiles - 3) // 2 + 1, n_steps):
        compose(k)
    const = jnp.zeros((1, width), F32)
    for k in range(n_steps):
        row = pl.ds(k, 1)
        own = known_ref[row, :] + keep_ref[row, :] * (pm[row, :] / (2.0 * (width + 1.0)))
        free[row, :] = own
        const = row_times(columns_of(const - mean_ref[row, :]), lambda r, c: jac[k, r, c]) + own
    last[pl.ds(width, 8), :] = jnp.concatenate([const, jnp.zeros((7, width), F32)], axis=0)
    first[...] = row_times(columns_of(start[...]), lambda r, c: last[r, c]) + const
    for send in sends:
        send.wait()


def fetch_kernel(count, *refs):
    sources, targets, sems = refs[:count], refs[-1 - count : -1], refs[-1]
    copies = [
        pltpu.make_async_copy(source, target, sems.at[i])
        for i, (source, target) in enumerate(zip(sources, targets))
    ]
    for copy in copies:
        copy.start()
    for copy in copies:
        copy.wait()


def fetch(arrays, after=()):
    return pl.pallas_call(
        functools.partial(fetch_kernel, len(arrays)),
        out_shape=tuple(jax.ShapeDtypeStruct(x.shape, x.dtype) for x in arrays),
        in_specs=[HBM] * len(arrays) + [VMEM] * len(after),
        out_specs=(VMEM,) * len(arrays),
        scratch_shapes=[pltpu.SemaphoreType.DMA((len(arrays),))],
        compiler_params=params(16),
    )(*arrays, *after)


def first_kernel(late, entry, leaving):
    width = late.shape[1]
    leaving[...] = row_times(columns_of(entry[...]), lambda r, c: late[r, c]) + late[pl.ds(width, 1), :]


def second_kernel(early, late, held, moved, entry, leaving):
    width = late.shape[1]
    row = jnp.where(lax.axis_index("tm") == 3, moved[...], held[...])
    entry[...] = row
    mid = row_times(columns_of(row), lambda r, c: early[r, c]) + early[pl.ds(width, 1), :]
    leaving[...] = row_times(columns_of(mid), lambda r, c: late[r, c]) + late[pl.ds(width, 1), :]


def pair_kernel(early, late, chip):
    width = late.shape[1]
    both = product(early[...], late[pl.ds(0, width), :])
    chip[pl.ds(0, width), :] = both[:width]
    const = both[width : width + 1] + late[pl.ds(width, 1), :]
    chip[pl.ds(width, 8), :] = jnp.broadcast_to(const, (8, width))


def hop_kernel(chip_at, chip, held, moved, *refs):
    entry, leaving = refs[-2:]
    width = chip.shape[1]
    arrived = lax.axis_index("tm") == 2 * chip_at + 1
    row = jnp.where(arrived, moved[...], held[...])
    entry[...] = row
    leaving[...] = row_times(columns_of(row), lambda r, c: chip[r, c]) + chip[pl.ds(width, 1), :]


def arrive_kernel(chip_at, held, moved, entry):
    entry[...] = jnp.where(lax.axis_index("tm") == 2 * chip_at + 1, moved[...], held[...])


def final_kernel(chosen, early, steps, last, free, mean, entry, other, *refs):
    out, rows, sem = refs[-3:]
    n_steps, width = free.shape
    place = lax.axis_index("tm")

    @pl.when(chosen(place // 2))
    def _():
        mid = row_times(columns_of(entry[...]), lambda r, c: early[r, c]) + early[pl.ds(width, 1), :]
        state = jnp.where(place % 2 == 1, mid, other[...])
        rows[pl.ds(n_steps - 1, 1), :] = (
            row_times(columns_of(state), lambda r, c: last[r, c]) + last[pl.ds(width, 1), :]
        )
        for k in range(n_steps - 1):
            row = pl.ds(k, 1)
            state = row_times(columns_of(state - mean[row, :]), lambda r, c: steps[k, r, c]) + free[row, :]
            rows[row, :] = state
        copy = pltpu.make_async_copy(rows, out, sem)
        copy.start()
        copy.wait()


def params(mib):
    return pltpu.CompilerParams(vmem_limit_bytes=mib * 1024 * 1024)


def body(lin_mean, spread, keep, observed, start, w_in, b_in, w_out, b_out):
    n_steps, width = lin_mean.shape
    units = w_in.shape[1]
    size = lax.axis_size("tm")
    shape = jax.ShapeDtypeStruct

    small = pltpu.VMEM((n_steps, width), F32)
    row = start.reshape(1, width)
    steps, last, free, first = pl.pallas_call(
        net_kernel,
        out_shape=(
            shape((n_steps - 1, width, width), F32),
            shape((width + 8, width), F32),
            shape((n_steps, width), F32),
            shape((1, width), F32),
        ),
        in_specs=[HBM] * 9,
        out_specs=(HBM, VMEM, VMEM, VMEM),
        scratch_shapes=[
            small, small, small, small,
            pltpu.VMEM((1, units), F32),
            pltpu.VMEM((1, width), F32),
            pltpu.VMEM((1, width), F32),
            pltpu.VMEM((width, units), BF16),
            pltpu.VMEM((units, width), BF16),
            pltpu.VMEM((width, LANES), F32),
            pltpu.VMEM((width, units), F32),
            pltpu.VMEM((n_steps, units), F32),
            pltpu.VMEM((4, n_steps, width, LANES), F32),
            pltpu.VMEM((width, units), BF16),
            pltpu.VMEM((width, units), BF16),
            pltpu.VMEM((n_steps, width, width), F32),
            pltpu.VMEM((8, width), F32),
            pltpu.VMEM((8, width), F32),
            pltpu.VMEM((n_steps - 1, width, width), F32),
            pltpu.SemaphoreType.DMA((12,)),
            pltpu.SemaphoreType.DMA((n_steps,)),
        ],
        compiler_params=params(60),
    )(lin_mean, spread, keep, observed, b_in.reshape(1, units), b_out.reshape(1, width), row, w_in, w_out)

    swap = [(i, i ^ 1) for i in range(size)]
    halfway = lax.ppermute(first, "tm", swap)
    (late,) = fetch((last,))
    (sent,) = fetch((late,), (halfway,))
    early = lax.ppermute(sent, "tm", swap)
    leaving = pl.pallas_call(
        first_kernel,
        out_shape=shape((1, width), F32),
        in_specs=[VMEM] * 2,
        out_specs=VMEM,
        compiler_params=params(16),
    )(late, halfway)
    chip = pl.pallas_call(
        pair_kernel,
        out_shape=shape((width + 8, width), F32),
        in_specs=[VMEM] * 2,
        out_specs=VMEM,
        compiler_params=params(16),
    )(early, late)
    row_shape = shape((1, width), F32)
    chips = size // 2
    kept = ()

    def finish(chosen, entry, other, kept):
        return pl.pallas_call(
            functools.partial(final_kernel, chosen),
            out_shape=shape((n_steps, width), F32),
            in_specs=[VMEM] * 7 + [HBM] * len(kept),
            out_specs=HBM,
            input_output_aliases={7: 0} if kept else {},
            scratch_shapes=[pltpu.VMEM((n_steps, width), F32), pltpu.SemaphoreType.DMA],
            compiler_params=params(16),
        )(early, steps, late, free, lin_mean, entry, other, *kept)

    entry = row
    for chip_at in range(1, chips):
        if chip_at % 2 == 1 and size % 4 == 0:
            moved = lax.ppermute(leaving, "tm", [(i, i ^ 2) for i in range(size)])
        else:
            moved = lax.ppermute(leaving, "tm", [(2 * chip_at - 1, 2 * chip_at + 1)])
        ready = (free,) if chip_at == 2 else ()
        if chip_at == 1:
            steps, free, lin_mean = fetch((steps, free, lin_mean), (moved,))
        if chip_at == 1 and chips > 2:
            entry, leaving = pl.pallas_call(
                second_kernel,
                out_shape=(row_shape, row_shape),
                in_specs=[VMEM] * 4,
                out_specs=(VMEM, VMEM),
                compiler_params=params(16),
            )(early, late, entry, moved)
        elif chip_at < chips - 1:
            entry, leaving = pl.pallas_call(
                functools.partial(hop_kernel, chip_at),
                out_shape=(row_shape, row_shape),
                in_specs=[VMEM] * (3 + len(ready)),
                out_specs=(VMEM, VMEM),
                compiler_params=params(16),
            )(chip, entry, moved, *ready)
        else:
            other = lax.ppermute(entry, "tm", swap)
            kept = (finish(lambda at: at < chips - 1, entry, other, ()),)
            entry = pl.pallas_call(
                functools.partial(arrive_kernel, chip_at),
                out_shape=row_shape,
                in_specs=[VMEM] * 2,
                out_specs=VMEM,
                compiler_params=params(16),
            )(entry, moved)
    other = lax.ppermute(entry, "tm", swap)
    return finish(lambda at: at == chips - 1, entry, other, kept)


def solution(mesh):
    rows = P(("groups", "tm"), None)
    placed = (rows, rows, rows, rows, P("groups"), P(), P(), P(), P())
    return jax.shard_map(body, mesh=mesh, in_specs=placed, out_specs=rows, check_vma=False)
```

```python
import functools
import math

import jax
import jax.numpy as jnp
from jax import lax
from jax.experimental import pallas as pl
from jax.experimental.pallas import tpu as pltpu
from jax.sharding import PartitionSpec as P

C0 = math.sqrt(2.0 / math.pi)
C1 = 0.044715 * C0
LANES = 128
F32 = jnp.float32
BF16 = jnp.bfloat16
VMEM = pl.BlockSpec(memory_space=pltpu.VMEM)
HBM = pl.BlockSpec(memory_space=pltpu.HBM)


def split(x):
    hi = x.astype(BF16)
    return hi, (x - hi.astype(F32)).astype(BF16)


def product(left, right):
    lhi, llo = split(left)
    rhi, rlo = split(right)
    both = jnp.dot(jnp.concatenate([lhi, llo], axis=0), rhi, preferred_element_type=F32)
    rows = left.shape[0]
    return both[:rows] + both[rows:] + jnp.dot(lhi, rlo, preferred_element_type=F32)


def rows_times(row, *matrices):
    width = row.shape[1]
    totals = [[None] * (width // LANES) for _ in matrices]
    for b in range(0, width, LANES):
        column = jnp.transpose(jnp.broadcast_to(row[:, b : b + LANES], (LANES, LANES)))
        for total, matrix in zip(totals, matrices):
            for i, c in enumerate(range(0, width, LANES)):
                block = column * matrix(pl.ds(b, LANES), pl.ds(c, LANES))
                term = jnp.sum(block.reshape(LANES // 8, 8, LANES), axis=0)
                total[i] = term if total[i] is None else total[i] + term
    return [
        jnp.concatenate([jnp.sum(part, axis=0, keepdims=True) for part in total], axis=1) for total in totals
    ]


def row_times(row, matrix):
    return rows_times(row, matrix)[0]


def net_kernel(
    mean_h, spread_h, keep_h, obs_h, b_in_h, b_out_h, start_h, w_in_h, w_out_h,
    prefix, last, offsets, first,
    mean_ref, spread_ref, keep_ref, obs_ref, b_in, b_out, start, w_in, w_out,
    turned, w_wide, base, wide, h0, h1, jac, pm, known_ref, held_ref, sems, out_sems,
):
    n_steps, width = mean_ref.shape
    units = w_in.shape[1]
    half = width // 4
    per = width // half
    factor = math.sqrt(width + 1.0)
    sources = (mean_h, spread_h, keep_h, obs_h, b_in_h, b_out_h, start_h)
    targets = (mean_ref, spread_ref, keep_ref, obs_ref, b_in, b_out, start)
    copies = [
        pltpu.make_async_copy(source, target, sems.at[i])
        for i, (source, target) in enumerate(zip(sources, targets))
    ]
    quarter = units // 4
    for i in range(4):
        part = pl.ds(i * quarter, quarter)
        copies.append(pltpu.make_async_copy(w_in_h.at[:, part], w_in.at[:, part], sems.at[7 + i]))
    copies.append(pltpu.make_async_copy(w_out_h, w_out, sems.at[11]))
    for copy in copies:
        copy.start()
    for copy in copies[:7]:
        copy.wait()


    mean = mean_ref[...]
    centre_pts = mean.astype(BF16)
    centre_f = centre_pts.astype(F32)
    spread = spread_ref[...]
    up = (mean + factor * spread).astype(BF16).astype(F32)
    lo = (mean - factor * spread).astype(BF16).astype(F32)
    inv = 1.0 / (2.0 * factor * spread)
    eye = lax.broadcasted_iota(jnp.int32, (LANES, LANES), 0) == lax.broadcasted_iota(
        jnp.int32, (LANES, LANES), 1
    )
    kinds = (0.5 * (up - centre_f), 0.5 * (lo - centre_f), inv, (up - lo) * inv)
    stacked = jnp.concatenate(kinds + (jnp.zeros((LANES - 4 * n_steps, width), F32),), axis=0)
    for b in range(0, width, LANES):
        turned[pl.ds(b, LANES), :] = jnp.transpose(stacked[:, b : b + LANES])

    def widen(k, kinds):
        for b in range(0, width, LANES):
            for a in kinds:
                at = a * n_steps + k
                block = jnp.broadcast_to(turned[pl.ds(b, LANES), at : at + 1], (LANES, LANES))
                if a == 3:
                    block = jnp.where(eye, block, 0.0)
                wide[k][a // 2][a % 2, pl.ds(b, LANES), :] = block

    widen(0, (0, 1))

    def gelu(k, j0, dst):
        for c in range(0, units, 256):
            if k == 0 and j0 == 0 and c == 3 * quarter:
                copies[11].wait()
            if k == 0 and j0 == 0 and c % quarter == 0:
                copies[7 + c // quarter].wait()
                part = pl.ds(c, quarter)
                base[:, part] = (
                    jnp.dot(centre_pts, w_in[:, part], preferred_element_type=F32) + b_in[:, part]
                ) * 0.5
            b = base[pl.ds(k, 1), pl.ds(c, 256)]
            for r in range(0, half, 16):
                place = (pl.ds(j0 + r, 16), pl.ds(c, 256))
                if k == 0:
                    w = w_in[place].astype(F32)
                    w_wide[place] = w
                else:
                    w = w_wide[place]
                for s in range(2):
                    d = wide[k][0][s, pl.ds(j0 + r, 16), :]
                    y = b + jnp.concatenate([d, d], axis=1) * w
                    z = y * (y * y * (8.0 * C1) + 2.0 * C0)
                    dst[pl.ds(s * half + r, 16), pl.ds(c, 256)] = (y * jnp.tanh(z) + y).astype(BF16)

    def outer(k, j0, src):
        out = jnp.dot(src[...], w_out[...], preferred_element_type=F32)
        keep = keep_ref[pl.ds(k, 1), :]
        sums = []
        for c in range(0, width, LANES):
            upper, lower = out[:half, c : c + LANES], out[half:, c : c + LANES]
            for r in range(0, half, LANES):
                v = (upper[r : r + LANES] - lower[r : r + LANES]) * wide[k][1][0, pl.ds(j0 + r, LANES), :]
                if c == j0 + r:
                    v = v + wide[k][1][1, pl.ds(c, LANES), :]
                jac[k][pl.ds(j0 + r, LANES), pl.ds(c, LANES)] = v * keep[:, c : c + LANES]
            sums.append(jnp.sum(upper + lower, axis=0, keepdims=True))
        return jnp.concatenate(sums, axis=1)

    sends = []

    def compose(k):
        held = product((held_ref[k - 1] if k > 1 else jac[0])[...], jac[k][...])
        if k < n_steps - 1:
            held_ref[k][...] = held
        else:
            last[pl.ds(0, width), :] = held

    def send(k):
        source = held_ref[k] if k > 0 else jac[0]
        sends.append(pltpu.make_async_copy(source, prefix.at[k], out_sems.at[k]))
        sends[-1].start()

    points = 2.0 * width
    slots = (h0, h1)
    tiles = per * n_steps
    for tile in range(tiles + 1):
        if tile == tiles - 1:
            for k in range(n_steps - 2):
                send(k)
        if tile > 0:
            k, side = (tile - 1) // per, (tile - 1) % per
            total = outer(k, side * half, slots[(tile - 1) % 2])
            pm[pl.ds(k, 1), :] = total if side == 0 else pm[pl.ds(k, 1), :] + total
        if tile > 2 * per and tile % per == 1:
            compose(tile // per - 1)
        if tile < tiles:
            gelu(tile // per, (tile % per) * half, slots[tile % 2])
        if tile == 0:
            widen(0, (2, 3))
        if tile == 2:
            y = base[...]
            z = y * (y * y * (8.0 * C1) + 2.0 * C0)
            hidden = (y * jnp.tanh(z) + y).astype(BF16)
            centre = jnp.dot(hidden, w_out[...], preferred_element_type=F32) + b_out[...] + centre_f
            keep = keep_ref[...]
            known = keep * (
                centre / (width + 1.0)
                + (points * b_out[...] + ((points - 2.0) * centre_f + (up + lo))) / (2.0 * (width + 1.0))
            ) + (1.0 - keep) * obs_ref[...]
            known_ref[pl.ds(0, n_steps), :] = known
        if tile % per == 1 and tile + per < tiles:
            widen(tile // per + 1, (0, 1, 2, 3))
    send(n_steps - 2)
    compose(n_steps - 1)
    const = jnp.zeros((1, width), F32)
    for k in range(n_steps):
        row = pl.ds(k, 1)
        own = known_ref[row, :] + keep_ref[row, :] * (pm[row, :] / (2.0 * (width + 1.0)))
        const = row_times(const - mean_ref[row, :], lambda r, c: jac[k][r, c]) + own
        offsets[row, :] = const
    last[pl.ds(width, 8), :] = jnp.concatenate([const, jnp.zeros((7, width), F32)], axis=0)
    first[...] = row_times(start[...], lambda r, c: last[r, c]) + const
    for send in sends:
        send.wait()


def fetch_kernel(count, *refs):
    sources, targets, sems = refs[:count], refs[-1 - count : -1], refs[-1]
    copies = [
        pltpu.make_async_copy(source, target, sems.at[i])
        for i, (source, target) in enumerate(zip(sources, targets))
    ]
    for copy in copies:
        copy.start()
    for copy in copies:
        copy.wait()


def fetch(arrays, after=()):
    return pl.pallas_call(
        functools.partial(fetch_kernel, len(arrays)),
        out_shape=tuple(jax.ShapeDtypeStruct(x.shape, x.dtype) for x in arrays),
        in_specs=[HBM] * len(arrays) + [VMEM] * len(after),
        out_specs=(VMEM,) * len(arrays),
        scratch_shapes=[pltpu.SemaphoreType.DMA((len(arrays),))],
        compiler_params=params(16),
    )(*arrays, *after)


def first_kernel(late, entry, leaving):
    width = late.shape[1]
    leaving[...] = row_times(entry[...], lambda r, c: late[r, c]) + late[pl.ds(width, 1), :]


def second_kernel(early, late, held, moved, entry, leaving):
    width = late.shape[1]
    row = jnp.where(lax.axis_index("tm") == 3, moved[...], held[...])
    entry[...] = row
    mid = row_times(row, lambda r, c: early[r, c]) + early[pl.ds(width, 1), :]
    leaving[...] = row_times(mid, lambda r, c: late[r, c]) + late[pl.ds(width, 1), :]


def pair_kernel(early, late, chip):
    width = late.shape[1]
    both = product(early[...], late[pl.ds(0, width), :])
    chip[pl.ds(0, width), :] = both[:width]
    const = both[width : width + 1] + late[pl.ds(width, 1), :]
    chip[pl.ds(width, 8), :] = jnp.broadcast_to(const, (8, width))


def hop_kernel(chip_at, chip, held, moved, *refs):
    entry, leaving = refs[-2:]
    width = chip.shape[1]
    arrived = lax.axis_index("tm") == 2 * chip_at + 1
    row = jnp.where(arrived, moved[...], held[...])
    entry[...] = row
    leaving[...] = row_times(row, lambda r, c: chip[r, c]) + chip[pl.ds(width, 1), :]


def arrive_kernel(chip_at, held, moved, entry):
    entry[...] = jnp.where(lax.axis_index("tm") == 2 * chip_at + 1, moved[...], held[...])


def final_kernel(chosen, early, prefix, last, offsets, entry, other, *refs):
    out, rows, sem = refs[-3:]
    n_steps, width = offsets.shape
    place = lax.axis_index("tm")

    @pl.when(chosen(place // 2))
    def _():
        mid = row_times(entry[...], lambda r, c: early[r, c]) + early[pl.ds(width, 1), :]
        state = jnp.where(place % 2 == 1, mid, other[...])
        loads = [lambda r, c, k=k: prefix[k, r, c] for k in range(n_steps - 1)]
        moved = rows_times(state, *loads, lambda r, c: last[r, c])
        rows[...] = jnp.concatenate(moved, axis=0) + offsets[...]
        copy = pltpu.make_async_copy(rows, out, sem)
        copy.start()
        copy.wait()


def params(mib):
    return pltpu.CompilerParams(vmem_limit_bytes=mib * 1024 * 1024)


def body(lin_mean, spread, keep, observed, start, w_in, b_in, w_out, b_out):
    n_steps, width = lin_mean.shape
    units = w_in.shape[1]
    size = lax.axis_size("tm")
    shape = jax.ShapeDtypeStruct

    small = pltpu.VMEM((n_steps, width), F32)
    row = start.reshape(1, width)
    prefix, last, offsets, first = pl.pallas_call(
        net_kernel,
        out_shape=(
            shape((n_steps - 1, width, width), F32),
            shape((width + 8, width), F32),
            shape((n_steps, width), F32),
            shape((1, width), F32),
        ),
        in_specs=[HBM] * 9,
        out_specs=(HBM, VMEM, VMEM, VMEM),
        scratch_shapes=[
            small, small, small, small,
            pltpu.VMEM((1, units), F32),
            pltpu.VMEM((1, width), F32),
            pltpu.VMEM((1, width), F32),
            pltpu.VMEM((width, units), BF16),
            pltpu.VMEM((units, width), BF16),
            pltpu.VMEM((width, LANES), F32),
            pltpu.VMEM((width, units), F32),
            pltpu.VMEM((n_steps, units), F32),
            [[pltpu.VMEM((2, width, LANES), F32)] * 2] * n_steps,
            pltpu.VMEM((width // 2, units), BF16),
            pltpu.VMEM((width // 2, units), BF16),
            [pltpu.VMEM((width, width), F32)] * n_steps,
            pltpu.VMEM((8, width), F32),
            pltpu.VMEM((8, width), F32),
            [pltpu.VMEM((width, width), F32)] * (n_steps - 1),
            pltpu.SemaphoreType.DMA((12,)),
            pltpu.SemaphoreType.DMA((n_steps,)),
        ],
        compiler_params=params(60),
    )(lin_mean, spread, keep, observed, b_in.reshape(1, units), b_out.reshape(1, width), row, w_in, w_out)

    swap = [(i, i ^ 1) for i in range(size)]
    halfway = lax.ppermute(first, "tm", swap)
    (late,) = fetch((last,))
    (sent,) = fetch((late,), (halfway,))
    early = lax.ppermute(sent, "tm", swap)
    leaving = pl.pallas_call(
        first_kernel,
        out_shape=shape((1, width), F32),
        in_specs=[VMEM] * 2,
        out_specs=VMEM,
        compiler_params=params(16),
    )(late, halfway)
    chip = pl.pallas_call(
        pair_kernel,
        out_shape=shape((width + 8, width), F32),
        in_specs=[VMEM] * 2,
        out_specs=VMEM,
        compiler_params=params(16),
    )(early, late)
    row_shape = shape((1, width), F32)
    chips = size // 2
    kept = ()

    def finish(chosen, entry, other, kept):
        return pl.pallas_call(
            functools.partial(final_kernel, chosen),
            out_shape=shape((n_steps, width), F32),
            in_specs=[VMEM] * 6 + [HBM] * len(kept),
            out_specs=HBM,
            input_output_aliases={6: 0} if kept else {},
            scratch_shapes=[pltpu.VMEM((n_steps, width), F32), pltpu.SemaphoreType.DMA],
            compiler_params=params(16),
        )(early, prefix, late, offsets, entry, other, *kept)

    entry = row
    for chip_at in range(1, chips):
        if chip_at % 2 == 1 and size % 4 == 0:
            moved = lax.ppermute(leaving, "tm", [(i, i ^ 2) for i in range(size)])
        else:
            moved = lax.ppermute(leaving, "tm", [(2 * chip_at - 1, 2 * chip_at + 1)])
        ready = (offsets,) if chip_at == 2 else ()
        if chip_at == 1:
            prefix, offsets = fetch((prefix, offsets), (moved,))
        if chip_at == 1 and chips > 2:
            entry, leaving = pl.pallas_call(
                second_kernel,
                out_shape=(row_shape, row_shape),
                in_specs=[VMEM] * 4,
                out_specs=(VMEM, VMEM),
                compiler_params=params(16),
            )(early, late, entry, moved)
        elif chip_at < chips - 1:
            entry, leaving = pl.pallas_call(
                functools.partial(hop_kernel, chip_at),
                out_shape=(row_shape, row_shape),
                in_specs=[VMEM] * (3 + len(ready)),
                out_specs=(VMEM, VMEM),
                compiler_params=params(16),
            )(chip, entry, moved, *ready)
        else:
            other = lax.ppermute(entry, "tm", swap)
            kept = (finish(lambda at: at < chips - 1, entry, other, ()),)
            entry = pl.pallas_call(
                functools.partial(arrive_kernel, chip_at),
                out_shape=row_shape,
                in_specs=[VMEM] * 2,
                out_specs=VMEM,
                compiler_params=params(16),
            )(entry, moved)
    other = lax.ppermute(entry, "tm", swap)
    return finish(lambda at: at == chips - 1, entry, other, kept)


def solution(mesh):
    rows = P(("groups", "tm"), None)
    placed = (rows, rows, rows, rows, P("groups"), P(), P(), P(), P())
    return jax.shard_map(body, mesh=mesh, in_specs=placed, out_specs=rows, check_vma=False)
```
